32 devices in a mesh: blk: 32 (over z, y, x, core).
Axes of the slice: x: 2, y: 2, z: 4, core: 2. Of those that a mesh axis runs over, the one named last changes fastest.
Arguments:
- raw_tiles: bfloat16 [256, 64, 384], P('blk'), may hold values from -6 to 6
- flat_field: bfloat16 [32, 64, 384], P('blk'), may hold values from 0.5 to 2
- dark_field: bfloat16 [32, 64, 384], P('blk'), may hold values from -3 to 3
- blend_ramp: int32 [32, 384], P('blk'), may hold values from 1 to 65
- source_used: int32 [32, 5], P('blk'), may hold values from 0 to 1, as said below
- source_offset: int32 [32, 5], P('blk'), may hold values from 0 to 128
Outputs:
- volume: float32 [256, 64, 256], P('blk')
The draws below stay inside these ranges and needn't reach their ends.
Inputs may be any that keep to these rules, and one draw needn't show every extreme that they name: source_used[b, 2] is 1 for every block, and no used slot names a tile outside 0..31.
All inputs are finite; a program needn't handle non-finite values.
Results may differ from the reference program's by a relative error of at most 0.0003.
Values may be sent and summed in bfloat16 or wider, within the bound.
A program may use at most 64 MiB of HBM per device.

```python
import math
import jax
import jax.numpy as jnp
from jax import lax

BZ = 8
BY = 64
BX = 256
OFF = 128
XT = 384
NB = 32


def choose_full(key):
    return jax.random.randint(jax.random.fold_in(key, 7), (), 2, NB - 2)


def draw_source_used(key, part):
    blocks = jnp.arange(NB, dtype=jnp.int32)[:, None]
    deltas = jnp.arange(5, dtype=jnp.int32)[None, :] - 2
    coins = jax.random.randint(jax.random.fold_in(key, 11), (NB, 5), 0, 2)
    inside = ((blocks + deltas >= 0) & (blocks + deltas < NB)).astype(jnp.int32)
    chosen = jnp.where(deltas == 0, 1, coins * inside)
    full_block = choose_full(key)
    chosen = jnp.where(blocks == full_block, 1, chosen)
    return chosen.astype(jnp.int32)


def draw_source_offset(key, part):
    blocks = jnp.arange(NB, dtype=jnp.int32)[:, None]
    deltas = jnp.arange(5, dtype=jnp.int32)[None, :] - 2
    offsets = jax.random.randint(jax.random.fold_in(key, 13), (NB, 5), 0, OFF + 1)
    full_block = choose_full(key)
    offsets = jnp.where((blocks == full_block) & (deltas == 0), OFF, offsets)
    offsets = jnp.where((blocks == full_block) & (deltas == 1), 0, offsets)
    return offsets.astype(jnp.int32)


def draw_blend_ramp(key, part):
    rise = jax.random.randint(jax.random.fold_in(key, 17), (NB, 1), 16, 129)
    columns = jnp.arange(XT, dtype=jnp.int32)[None, :]
    distance = jnp.minimum(jnp.minimum(columns, XT - 1 - columns), rise)
    noise = jax.random.randint(jax.random.fold_in(key, 19), (NB, XT), 0, 2)
    ramp_values = 1 + distance * 63 // rise + noise
    ramp_values = ramp_values.at[0, 0].set(1)
    ramp_values = ramp_values.at[0, XT // 2].set(65)
    return ramp_values.astype(jnp.int32)


def block_levels(rng, extent, split, low, largest):
    loudness, own = 1.0, jax.random.fold_in(rng, 6)
    for dim, parts in split:
        heights = jnp.exp(jax.random.uniform(jax.random.fold_in(own, dim), (parts,), jnp.float32, low / len(split), largest / len(split)))
        loudness = loudness * jnp.repeat(heights, extent[dim] // parts).reshape([-1 if axis == dim else 1 for axis in range(len(extent))])
    return loudness


def scatter_about(own_key, dims, scale, reach, pieces=(), held_as=jnp.bfloat16):
    result = jax.random.normal(own_key, dims, jnp.float32) * scale
    if len(pieces) > 0:
        result = block_levels(own_key, dims, pieces, -0.22, 0.18) * result
    return jnp.clip(result, min=-reach, max=reach).astype(held_as)


def setup_inputs(seed: int = 0) -> dict:
    keys = jax.random.split(jax.random.key(seed), 7)
    raw_tiles = scatter_about(keys[0], (NB * BZ, BY, XT), 1.0, 6.0, ((0, 32),))
    flat_field = jnp.clip(jnp.exp(math.log(2.0) - 1.3862944 * jax.random.uniform(keys[1], (NB, BY, XT), jnp.float32) ** block_levels(keys[1], (NB, BY, XT), ((0, 32),), -0.2, 0.2)), 0.5, 2.0).astype(jnp.bfloat16)
    dark_field = scatter_about(keys[2], (NB, BY, XT), 0.5, 3.0, ((0, 32),))
    blend_ramp = draw_blend_ramp(jax.random.fold_in(keys[6], 71), 0)
    source_used = draw_source_used(jax.random.fold_in(keys[6], 71), 0)
    source_offset = draw_source_offset(jax.random.fold_in(keys[6], 71), 0)
    return {"raw_tiles": raw_tiles, "flat_field": flat_field, "dark_field": dark_field, "blend_ramp": blend_ramp, "source_used": source_used, "source_offset": source_offset}


thresholds = (1.0, 0.8, 0.6, 0.5)


def correct(camera, flat_gain, dark_level):
    return (camera.astype(jnp.float32) - dark_level.astype(jnp.float32)) / flat_gain.astype(jnp.float32)


def diffuse(extended, kappa_value):
    padded = jnp.pad(extended, ((0, 0), (1, 1), (1, 1)), mode="edge")
    center = padded[1:-1, 1:-1, 1:-1]
    others = [padded[2:, 1:-1, 1:-1], padded[:-2, 1:-1, 1:-1], padded[1:-1, 2:, 1:-1],
              padded[1:-1, :-2, 1:-1], padded[1:-1, 1:-1, 2:], padded[1:-1, 1:-1, :-2]]
    flux_sum = jnp.zeros(center.shape, jnp.float32)
    for neighbour in others:
        gradient = neighbour - center
        scaled = gradient / kappa_value
        flux_sum = flux_sum + gradient / (1.0 + scaled * scaled)
    return center + 0.12 * flux_sum


def reference(raw_tiles, flat_field, dark_field, blend_ramp, source_used, source_offset):
    camera_tiles = raw_tiles.reshape(NB, BZ, BY, XT)

    def join_block(block_id):
        numerator = jnp.zeros((BZ, BY, BX), jnp.float32)
        denominator = jnp.zeros((BX,), jnp.float32)
        for slot_id in range(5):
            source = jnp.clip(block_id + slot_id - 2, 0, NB - 1).astype(jnp.int32)
            corrected = correct(camera_tiles[source], flat_field[source][None], dark_field[source][None])
            offset = source_offset[block_id, slot_id].astype(jnp.int32)
            window = lax.dynamic_slice_in_dim(corrected, offset, BX, 2)
            weights = lax.dynamic_slice_in_dim(blend_ramp[source].astype(jnp.float32), offset, BX, 0)
            taken = source_used[block_id, slot_id] == 1
            numerator = numerator + jnp.where(taken, window * weights, jnp.float32(0.0))
            denominator = denominator + jnp.where(taken, weights, jnp.float32(0.0))
        return numerator / denominator

    joined_blocks = lax.map(join_block, jnp.arange(NB, dtype=jnp.int32))
    volume = joined_blocks.reshape(NB * BZ, BY, BX)
    for kappa_value in thresholds:
        extended = jnp.pad(volume, ((1, 1), (0, 0), (0, 0)), mode="edge")
        volume = diffuse(extended, kappa_value)
    return volume
```

```python
import functools

import jax
import jax.numpy as jnp
from jax import lax
from jax.experimental import pallas as pl
from jax.experimental.pallas import tpu as pltpu
from jax.sharding import PartitionSpec as P

BX = 256
LANES = 128
LEVELS = 32767.0
thresholds = (1.0, 0.8, 0.6, 0.5)
HALO = len(thresholds)
MESH = pl.DeviceIdType.MESH


def window(array, offset):
    shift = (LANES - offset) & (LANES - 1)
    parts = [
        pltpu.roll(array[:, LANES * j : LANES * (j + 1)], shift, 1)
        for j in range(BX // LANES + 1)
    ]
    lane = lax.broadcasted_iota(jnp.int32, parts[0].shape, 1)
    inside = lane < LANES - offset
    return jnp.concatenate(
        [jnp.where(inside, parts[j], parts[j + 1]) for j in range(BX // LANES)], axis=1
    )


def quotient(difference, square):
    bottom = square + difference * difference
    guess = pl.reciprocal(bottom, approx=True)
    return difference * (guess * (2.0 - bottom * guess))


def kernel(
    n, raw, flat, dark, ramp, used, off, out,
    praw, pflat, pdark, pramp, fused, foff, nused, noff,
    corr, pcorr, qf, qn, rf, rn, sf, sn, rsf, rsn, u, send, recv,
):
    depth, rows = raw.shape[0], raw.shape[1]
    half = depth // 2
    me = lax.axis_index("blk")
    s = 2 * lax.rem(me, 2) - 1
    partner, near, far, far_from = me - s, me + s, me + 2 * s, me - 2 * s

    def inside(device):
        return jnp.logical_and(device >= 0, device < n)

    has_near, has_far, has_far_from = inside(near), inside(far), inside(far_from)
    has_below, has_above = me > 0, me < n - 1

    barrier = pltpu.get_barrier_semaphore()

    def greet(device):
        pl.semaphore_signal(barrier, inc=1, device_id=(device,), device_id_type=MESH)

    greet(partner)
    for device, there in ((near, has_near), (far, has_far), (far_from, has_far_from)):
        pl.when(there)(functools.partial(greet, device))
    pl.semaphore_wait(
        barrier,
        1
        + has_near.astype(jnp.int32)
        + has_far.astype(jnp.int32)
        + has_far_from.astype(jnp.int32),
    )

    def copy(number, source, target, device):
        return pltpu.make_async_remote_copy(
            src_ref=source,
            dst_ref=target,
            send_sem=send.at[number],
            recv_sem=recv.at[number],
            device_id=(device,),
            device_id_type=MESH,
        )

    meta_far = [copy(4, used, fused, far_from), copy(5, off, foff, far_from)]
    meta_near = [copy(6, used, nused, near), copy(7, off, noff, near)]
    tile = [
        copy(3, ramp, pramp, partner),
        copy(1, flat, pflat, partner),
        copy(2, dark, pdark, partner),
        copy(0, raw, praw, partner),
    ]

    def part(ref, chunk):
        return ref.at[pl.ds(chunk * half, half)]

    to_far = [copy(8 + c, part(qf, c), part(rf, c), far) for c in range(2)]
    to_far.append(copy(10, sf, rsf, far))
    to_near = [copy(11 + c, part(qn, c), part(rn, c), near) for c in range(2)]
    to_near.append(copy(13, sn, rsn, near))
    down = copy(14, u.at[pl.ds(HALO, HALO)], u.at[pl.ds(HALO + depth, HALO)], me - 1)
    up = copy(15, u.at[pl.ds(depth, HALO)], u.at[pl.ds(0, HALO)], me + 1)

    @pl.when(has_far_from)
    def _():
        for c in meta_far:
            c.start()

    @pl.when(has_near)
    def _():
        for c in meta_near:
            c.start()

    for c in tile:
        c.start()

    def corrected(raw_ref, flat_ref, dark_ref, target):
        inverse = 1.0 / flat_ref[0].astype(jnp.float32)
        level = dark_ref[0].astype(jnp.float32)

        def body(z, largest):
            value = (raw_ref[z].astype(jnp.float32) - level) * inverse
            target[z] = value
            return jnp.maximum(
                largest, jnp.max(jnp.abs(value).reshape(rows // 8, 8, -1), axis=0)
            )

        largest = lax.fori_loop(
            0, depth, body, jnp.zeros((8, raw_ref.shape[2]), jnp.float32)
        )
        return jnp.broadcast_to(
            jnp.max(largest, axis=0, keepdims=True), largest.shape
        )

    def weight(ramp_ref, taken, offset):
        row = jnp.broadcast_to(ramp_ref[...].astype(jnp.float32), (8, ramp_ref.shape[1]))
        return jnp.where(taken == 1, window(row, offset), 0.0)

    def levels(largest):
        return jnp.where(largest > 1e-30, LEVELS / jnp.maximum(largest, 1e-30), 0.0)

    def coded(value):
        return jnp.round(value).astype(jnp.int32).astype(jnp.int16)

    largest = corrected(raw, flat, dark, corr)

    @pl.when(has_far)
    def _():
        for c in meta_far:
            c.wait_recv()
        slot = 2 - 2 * s
        offset = foff[0, slot]
        scale = window(largest, offset)
        w = weight(ramp, fused[0, slot], offset)
        sf[0:8] = w * scale * (1.0 / LEVELS)
        sf[8:16] = w
        to_far[2].start()
        gain = levels(scale)[0:1]
        for c in range(2):
            def body(z, _):
                qf[z] = coded(window(corr[z], offset) * gain)
                return 0

            lax.fori_loop(c * half, (c + 1) * half, body, 0)
            to_far[c].start()

    for c in tile:
        c.wait_recv()
    plargest = corrected(praw, pflat, pdark, pcorr)

    @pl.when(has_near)
    def _():
        for c in meta_near:
            c.wait_recv()
        own, other = 2 - s, 2 - 2 * s
        offset, poffset = noff[0, own], noff[0, other]
        w = weight(ramp, nused[0, own], offset)
        pw = weight(pramp, nused[0, other], poffset)
        total = w + pw
        scale = jnp.maximum(
            jnp.where(w > 0.0, window(largest, offset), 0.0),
            jnp.where(pw > 0.0, window(plargest, poffset), 0.0),
        )
        sn[0:8] = total * scale * (1.0 / LEVELS)
        sn[8:16] = total
        to_near[2].start()
        gain = levels(scale) / jnp.maximum(total, 1.0)
        a, b = (w * gain)[0:1], (pw * gain)[0:1]
        for c in range(2):
            def body(z, _):
                qn[z] = coded(
                    window(corr[z], offset) * a + window(pcorr[z], poffset) * b
                )
                return 0

            lax.fori_loop(c * half, (c + 1) * half, body, 0)
            to_near[c].start()

    offset, poffset = off[0, 2], off[0, 2 - s]
    w = weight(ramp, used[0, 2], offset)
    pw = weight(pramp, used[0, 2 - s], poffset)
    a, b = w[0:1], pw[0:1]

    def base(z, _):
        u[HALO + z] = window(corr[z], offset) * a + window(pcorr[z], poffset) * b
        return 0

    lax.fori_loop(0, depth, base, 0)

    @pl.when(jnp.logical_not(has_far_from))
    def _():
        rsf[...] = jnp.zeros_like(rsf)

    @pl.when(jnp.logical_not(has_near))
    def _():
        rsn[...] = jnp.zeros_like(rsn)

    @pl.when(jnp.logical_not(has_below))
    def _():
        u[0:HALO] = jnp.zeros((HALO,) + u.shape[1:], jnp.float32)

    @pl.when(jnp.logical_not(has_above))
    def _():
        u[HALO + depth :] = jnp.zeros((HALO,) + u.shape[1:], jnp.float32)

    pl.when(has_far_from)(to_far[2].wait_recv)
    pl.when(has_near)(to_near[2].wait_recv)
    inverse = 1.0 / (w + pw + rsf[8:16] + rsn[8:16])
    scale_f = (rsf[0:8] * inverse)[0:1]
    scale_n = (rsn[0:8] * inverse)[0:1]
    inverse = inverse[0:1]
    for c in range(2):
        pl.when(has_far_from)(to_far[c].wait_recv)
        pl.when(has_near)(to_near[c].wait_recv)

        def join(z, _):
            u[HALO + z] = (
                u[HALO + z] * inverse
                + rf[z].astype(jnp.float32) * scale_f
                + rn[z].astype(jnp.float32) * scale_n
            )
            return 0

        lax.fori_loop(c * half, (c + 1) * half, join, 0)
        if c == 0:
            pl.when(has_below)(down.start)
        else:
            pl.when(has_above)(up.start)

    pl.when(has_below)(down.wait_send)
    pl.when(has_above)(up.wait_send)
    pl.when(has_above)(down.wait_recv)
    pl.when(has_below)(up.wait_recv)

    y = lax.broadcasted_iota(jnp.int32, u.shape[1:], 0)
    x = lax.broadcasted_iota(jnp.int32, u.shape[1:], 1)
    for number, kappa in enumerate(thresholds):
        square = kappa * kappa
        first = number + 1
        last = 2 * HALO + depth - 1 - number
        final = number == len(thresholds) - 1

        def body(z, before, square=square, final=final):
            here, following = u[z], u[z + 1]
            closed = jnp.logical_or(
                jnp.logical_and(z == HALO - 1, jnp.logical_not(has_below)),
                jnp.logical_and(z == HALO + depth - 1, jnp.logical_not(has_above)),
            )
            keep = jnp.where(closed, 0.0, 1.0)
            after = quotient((following - here) * keep, square)
            step = pltpu.roll(here, rows - 1, 0) - here
            flow_y = quotient(jnp.where(y == rows - 1, 0.0, step), square)
            step = pltpu.roll(here, BX - 1, 1) - here
            flow_x = quotient(jnp.where(x == BX - 1, 0.0, step), square)
            flux = (
                (after - before)
                + (flow_y - pltpu.roll(flow_y, 1, 0))
                + (flow_x - pltpu.roll(flow_x, 1, 1))
            )
            value = here + (0.12 * square) * flux
            if final:
                out[z - HALO] = value
            else:
                u[z] = value
            return after

        keep = 1.0
        if final:
            keep = jnp.where(has_below, 1.0, 0.0)
        before = quotient((u[first] - u[first - 1]) * keep, square)
        lax.fori_loop(first, last, body, before)

    for c in tile:
        c.wait_send()

    @pl.when(has_far_from)
    def _():
        for c in meta_far:
            c.wait_send()

    @pl.when(has_near)
    def _():
        for c in meta_near + to_near:
            c.wait_send()

    @pl.when(has_far)
    def _():
        for c in to_far:
            c.wait_send()


def shards(raw, flat, dark, ramp, used, off):
    n = lax.axis_size("blk")
    depth, rows, columns = raw.shape
    vmem = pl.BlockSpec(memory_space=pltpu.VMEM)
    smem = pl.BlockSpec(memory_space=pltpu.SMEM)
    coded = pltpu.VMEM((depth, rows, BX), jnp.int16)
    side = pltpu.VMEM((16, BX), jnp.float32)
    tile = pltpu.VMEM(raw.shape, jnp.float32)
    meta = pltpu.SMEM(used.shape, jnp.int32)
    return pl.pallas_call(
        functools.partial(kernel, n),
        out_shape=jax.ShapeDtypeStruct((depth, rows, BX), jnp.float32),
        in_specs=[vmem, vmem, vmem, vmem, smem, smem],
        out_specs=vmem,
        scratch_shapes=[
            pltpu.VMEM(raw.shape, raw.dtype),
            pltpu.VMEM(flat.shape, flat.dtype),
            pltpu.VMEM(dark.shape, dark.dtype),
            pltpu.VMEM(ramp.shape, ramp.dtype),
            meta, meta, meta, meta,
            tile, tile, coded, coded, coded, coded, side, side, side, side,
            pltpu.VMEM((depth + 2 * HALO, rows, BX), jnp.float32),
            pltpu.SemaphoreType.DMA((16,)),
            pltpu.SemaphoreType.DMA((16,)),
        ],
        compiler_params=pltpu.CompilerParams(
            collective_id=0, has_side_effects=True, vmem_limit_bytes=24 * 2**20
        ),
        cost_estimate=pl.CostEstimate(
            flops=30 * 6 * depth * rows * BX, bytes_accessed=10**6, transcendentals=0
        ),
    )(raw, flat, dark, ramp, used, off)


def solution(mesh):
    return jax.shard_map(
        shards,
        mesh=mesh,
        in_specs=(
            P("blk", None, None),
            P("blk", None, None),
            P("blk", None, None),
            P("blk", None),
            P("blk", None),
            P("blk", None),
        ),
        out_specs=P("blk", None, None),
        check_vma=False,
    )
```

```python
import functools

import jax
import jax.numpy as jnp
from jax import lax
from jax.experimental import pallas as pl
from jax.experimental.pallas import tpu as pltpu
from jax.sharding import PartitionSpec as P

BX = 256
LANES = 128
LEVELS = 32767.0
thresholds = (1.0, 0.8, 0.6, 0.5)
HALO = len(thresholds)
MESH = pl.DeviceIdType.MESH


def window(array, offset):
    shift = (LANES - offset) & (LANES - 1)
    parts = [
        pltpu.roll(array[:, LANES * j : LANES * (j + 1)], shift, 1)
        for j in range(BX // LANES + 1)
    ]
    lane = lax.broadcasted_iota(jnp.int32, parts[0].shape, 1)
    inside = lane < LANES - offset
    return jnp.concatenate(
        [jnp.where(inside, parts[j], parts[j + 1]) for j in range(BX // LANES)], axis=1
    )


def quotient(difference, square):
    bottom = square + difference * difference
    guess = pl.reciprocal(bottom, approx=True)
    return difference * (guess * (2.0 - bottom * guess))


def kernel(
    n, graw, gflat, gdark, gramp, gused, goff, out,
    raw, flat, dark, ramp, used, off,
    praw, pflat, pdark, pramp, fused, foff, nused, noff,
    corr, pcorr, qf, qn, rf, rn, sf, sn, rsf, rsn,
    qh, rh, sh, rsh, saved, u, local, send, recv,
):
    depth, rows = raw.shape[0], raw.shape[1]
    half = depth // 2
    me = lax.axis_index("blk")
    s = 2 * lax.rem(me, 2) - 1
    partner, near, far, far_from = me - s, me + s, me + 2 * s, me - 2 * s

    def inside(device):
        return jnp.logical_and(device >= 0, device < n)

    has_near, has_far, has_far_from = inside(near), inside(far), inside(far_from)
    has_below, has_above = me > 0, me < n - 1

    fetched = [
        pltpu.make_async_copy(source, target, local.at[number])
        for number, (source, target) in enumerate(
            ((gflat, flat), (gdark, dark), (graw, raw), (gramp, ramp), (gused, used), (goff, off))
        )
    ]
    for c in fetched:
        c.start()

    barrier = pltpu.get_barrier_semaphore()

    def greet(device):
        pl.semaphore_signal(barrier, inc=1, device_id=(device,), device_id_type=MESH)

    greet(partner)
    for device, there in ((near, has_near), (far, has_far), (far_from, has_far_from)):
        pl.when(there)(functools.partial(greet, device))
    pl.semaphore_wait(
        barrier,
        1
        + has_near.astype(jnp.int32)
        + has_far.astype(jnp.int32)
        + has_far_from.astype(jnp.int32),
    )

    def copy(number, source, target, device):
        return pltpu.make_async_remote_copy(
            src_ref=source,
            dst_ref=target,
            send_sem=send.at[number],
            recv_sem=recv.at[number],
            device_id=(device,),
            device_id_type=MESH,
        )

    meta_far = [copy(4, gused, fused, far_from), copy(5, goff, foff, far_from)]
    meta_near = [copy(6, gused, nused, near), copy(7, goff, noff, near)]
    tile = [
        copy(3, gramp, pramp, partner),
        copy(1, gflat, pflat, partner),
        copy(2, gdark, pdark, partner),
        copy(0, graw, praw, partner),
    ]

    def part(ref, chunk):
        return ref.at[pl.ds(chunk * half, half)]

    to_far = [copy(8 + c, part(qf, c), part(rf, c), far) for c in range(2)]
    to_far.append(copy(10, sf, rsf, far))
    to_near = [copy(11 + c, part(qn, c), part(rn, c), near) for c in range(2)]
    to_near.append(copy(13, sn, rsn, near))
    halos = [
        [copy(14, qh.at[0], rh.at[1], me - 1), copy(15, sh.at[0], rsh.at[1], me - 1)],
        [copy(16, qh.at[1], rh.at[0], me + 1), copy(17, sh.at[1], rsh.at[0], me + 1)],
    ]

    @pl.when(has_far_from)
    def _():
        for c in meta_far:
            c.start()

    @pl.when(has_near)
    def _():
        for c in meta_near:
            c.start()

    for c in tile:
        c.start()

    def corrected(raw_ref, flat_ref, dark_ref, target):
        inverse = 1.0 / flat_ref[0].astype(jnp.float32)
        level = dark_ref[0].astype(jnp.float32)

        def body(z, largest):
            value = (raw_ref[z].astype(jnp.float32) - level) * inverse
            target[z] = value
            return jnp.maximum(
                largest, jnp.max(jnp.abs(value).reshape(rows // 8, 8, -1), axis=0)
            )

        largest = lax.fori_loop(
            0, depth, body, jnp.zeros((8, raw_ref.shape[2]), jnp.float32)
        )
        return jnp.broadcast_to(
            jnp.max(largest, axis=0, keepdims=True), largest.shape
        )

    def weight(ramp_ref, taken, offset):
        row = jnp.broadcast_to(ramp_ref[...].astype(jnp.float32), (8, ramp_ref.shape[1]))
        return jnp.where(taken == 1, window(row, offset), 0.0)

    def levels(largest):
        return jnp.where(largest > 1e-30, LEVELS / jnp.maximum(largest, 1e-30), 0.0)

    def coded(value):
        return jnp.round(value).astype(jnp.int32).astype(jnp.int16)

    for c in fetched:
        c.wait()
    largest = corrected(raw, flat, dark, corr)

    @pl.when(has_far)
    def _():
        for c in meta_far:
            c.wait_recv()
        slot = 2 - 2 * s
        offset = foff[0, slot]
        scale = window(largest, offset)
        w = weight(ramp, fused[0, slot], offset)
        sf[0:8] = w * scale * (1.0 / LEVELS)
        sf[8:16] = w
        to_far[2].start()
        gain = levels(scale)[0:1]
        for c in range(2):
            def body(z, _):
                qf[z] = coded(window(corr[z], offset) * gain)
                return 0

            lax.fori_loop(c * half, (c + 1) * half, body, 0)
            to_far[c].start()

    for c in tile:
        c.wait_recv()
    plargest = corrected(praw, pflat, pdark, pcorr)

    @pl.when(has_near)
    def _():
        for c in meta_near:
            c.wait_recv()
        own, other = 2 - s, 2 - 2 * s
        offset, poffset = noff[0, own], noff[0, other]
        w = weight(ramp, nused[0, own], offset)
        pw = weight(pramp, nused[0, other], poffset)
        total = w + pw
        scale = jnp.maximum(
            jnp.where(w > 0.0, window(largest, offset), 0.0),
            jnp.where(pw > 0.0, window(plargest, poffset), 0.0),
        )
        sn[0:8] = total * scale * (1.0 / LEVELS)
        sn[8:16] = total
        to_near[2].start()
        gain = levels(scale) / jnp.maximum(total, 1.0)
        a, b = (w * gain)[0:1], (pw * gain)[0:1]
        for c in range(2):
            def body(z, _):
                qn[z] = coded(
                    window(corr[z], offset) * a + window(pcorr[z], poffset) * b
                )
                return 0

            lax.fori_loop(c * half, (c + 1) * half, body, 0)
            to_near[c].start()

    offset, poffset = off[0, 2], off[0, 2 - s]
    w = weight(ramp, used[0, 2], offset)
    pw = weight(pramp, used[0, 2 - s], poffset)
    a, b = w[0:1], pw[0:1]

    def base(z, _):
        u[HALO + z] = window(corr[z], offset) * a + window(pcorr[z], poffset) * b
        return 0

    lax.fori_loop(0, depth, base, 0)

    @pl.when(jnp.logical_not(has_far_from))
    def _():
        rsf[...] = jnp.zeros_like(rsf)

    @pl.when(jnp.logical_not(has_near))
    def _():
        rsn[...] = jnp.zeros_like(rsn)

    @pl.when(jnp.logical_not(has_below))
    def _():
        u[0:HALO] = jnp.zeros((HALO,) + u.shape[1:], jnp.float32)

    @pl.when(jnp.logical_not(has_above))
    def _():
        u[HALO + depth :] = jnp.zeros((HALO,) + u.shape[1:], jnp.float32)

    pl.when(has_far_from)(to_far[2].wait_recv)
    pl.when(has_near)(to_near[2].wait_recv)
    inverse = 1.0 / (w + pw + rsf[8:16] + rsn[8:16])
    scale_f = (rsf[0:8] * inverse)[0:1]
    scale_n = (rsn[0:8] * inverse)[0:1]
    inverse = inverse[0:1]
    for c in range(2):
        pl.when(has_far_from)(to_far[c].wait_recv)
        pl.when(has_near)(to_near[c].wait_recv)

        def join(z, largest):
            value = (
                u[HALO + z] * inverse
                + rf[z].astype(jnp.float32) * scale_f
                + rn[z].astype(jnp.float32) * scale_n
            )
            u[HALO + z] = value
            return jnp.maximum(
                largest, jnp.max(jnp.abs(value).reshape(rows // 8, 8, -1), axis=0)
            )

        largest = lax.fori_loop(
            c * half, (c + 1) * half, join, jnp.zeros((8, BX), jnp.float32)
        )

        @pl.when((has_below, has_above)[c])
        def _():
            scale = jnp.max(largest, axis=0, keepdims=True)
            sh[c] = jnp.broadcast_to(scale * (1.0 / LEVELS), (8, BX))
            gain = levels(scale)
            start = c * (depth - HALO)

            def code(z, _):
                qh[c, z] = coded(u[HALO + start + z] * gain)
                return 0

            lax.fori_loop(0, HALO, code, 0)
            for halo in halos[c]:
                halo.start()

    y = lax.broadcasted_iota(jnp.int32, u.shape[1:], 0)
    x = lax.broadcasted_iota(jnp.int32, u.shape[1:], 1)

    def stepped(here, before, after, square):
        step = pltpu.roll(here, rows - 1, 0) - here
        flow_y = quotient(jnp.where(y == rows - 1, 0.0, step), square)
        step = pltpu.roll(here, BX - 1, 1) - here
        flow_x = quotient(jnp.where(x == BX - 1, 0.0, step), square)
        flux = (
            (after - before)
            + (flow_y - pltpu.roll(flow_y, 1, 0))
            + (flow_x - pltpu.roll(flow_x, 1, 1))
        )
        return here + (0.12 * square) * flux

    planes = depth + 2 * HALO
    for number, kappa in enumerate(thresholds):
        square = kappa * kappa
        first, last = HALO + 1 + number, planes - HALO - 1 - number

        def body(z, before, square=square):
            here = u[z]
            after = quotient(u[z + 1] - here, square)
            u[z] = stepped(here, before, after, square)
            return after

        before = quotient(u[first] - u[first - 1], square)
        saved[0, number] = before
        saved[1, number] = -lax.fori_loop(first, last, body, before)

    lower_first = s > 0
    for turn in range(2):
        lower = lower_first if turn == 0 else jnp.logical_not(lower_first)
        side = jnp.where(lower, 0, 1)
        there = jnp.where(lower, has_below, has_above)
        origin = side * (planes - 1)
        sign = 1 - 2 * side

        @pl.when(jnp.logical_and(lower, has_below))
        def _():
            for halo in halos[1]:
                halo.wait_recv()

        @pl.when(jnp.logical_and(jnp.logical_not(lower), has_above))
        def _():
            for halo in halos[0]:
                halo.wait_recv()

        @pl.when(there)
        def _():
            scale = rsh[side, 0:1]

            def decode(z, _):
                u[side * (HALO + depth) + z] = rh[side, z].astype(jnp.float32) * scale
                return 0

            lax.fori_loop(0, HALO, decode, 0)

        open_face = jnp.where(there, 1.0, 0.0)
        for number, kappa in enumerate(thresholds):
            square = kappa * kappa
            final = number == HALO - 1

            def store(k, value, final=final):
                if final:
                    out[origin + sign * k - HALO] = value
                else:
                    u[origin + sign * k] = value

            def between(k, square=square):
                keep = jnp.where(k == HALO - 1, open_face, 1.0)
                return quotient(
                    (u[origin + sign * (k + 1)] - u[origin + sign * k]) * keep, square
                )

            def body(k, before, square=square, store=store, between=between):
                after = between(k)
                store(k, stepped(u[origin + sign * k], before, after, square))
                return after

            before = lax.fori_loop(
                number + 1, number + HALO, body, between(jnp.int32(number))
            )
            k = number + HALO
            store(
                k, stepped(u[origin + sign * k], before, saved[side, number], square)
            )

    @pl.when(has_below)
    def _():
        for halo in halos[0]:
            halo.wait_send()

    @pl.when(has_above)
    def _():
        for halo in halos[1]:
            halo.wait_send()

    for c in tile:
        c.wait_send()

    @pl.when(has_far_from)
    def _():
        for c in meta_far:
            c.wait_send()

    @pl.when(has_near)
    def _():
        for c in meta_near + to_near:
            c.wait_send()

    @pl.when(has_far)
    def _():
        for c in to_far:
            c.wait_send()


def shards(raw, flat, dark, ramp, used, off):
    n = lax.axis_size("blk")
    depth, rows, columns = raw.shape
    vmem = pl.BlockSpec(memory_space=pltpu.VMEM)
    coded = pltpu.VMEM((depth, rows, BX), jnp.int16)
    side = pltpu.VMEM((16, BX), jnp.float32)
    tile = pltpu.VMEM(raw.shape, jnp.float32)
    meta = pltpu.SMEM(used.shape, jnp.int32)
    held = [pltpu.VMEM(a.shape, a.dtype) for a in (raw, flat, dark, ramp)]
    return pl.pallas_call(
        functools.partial(kernel, n),
        out_shape=jax.ShapeDtypeStruct((depth, rows, BX), jnp.float32),
        in_specs=[pl.BlockSpec(memory_space=pl.ANY)] * 6,
        out_specs=vmem,
        scratch_shapes=[
            *held, meta, meta, *held, meta, meta, meta, meta,
            tile, tile, coded, coded, coded, coded, side, side, side, side,
            pltpu.VMEM((2, HALO, rows, BX), jnp.int16),
            pltpu.VMEM((2, HALO, rows, BX), jnp.int16),
            pltpu.VMEM((2, 8, BX), jnp.float32),
            pltpu.VMEM((2, 8, BX), jnp.float32),
            pltpu.VMEM((2, len(thresholds), rows, BX), jnp.float32),
            pltpu.VMEM((depth + 2 * HALO, rows, BX), jnp.float32),
            pltpu.SemaphoreType.DMA((6,)),
            pltpu.SemaphoreType.DMA((18,)),
            pltpu.SemaphoreType.DMA((18,)),
        ],
        compiler_params=pltpu.CompilerParams(
            collective_id=0, has_side_effects=True, vmem_limit_bytes=64 * 2**20 - 2**17
        ),
        cost_estimate=pl.CostEstimate(
            flops=30 * 6 * depth * rows * BX, bytes_accessed=10**6, transcendentals=0
        ),
    )(raw, flat, dark, ramp, used, off)


def solution(mesh):
    return jax.shard_map(
        shards,
        mesh=mesh,
        in_specs=(
            P("blk", None, None),
            P("blk", None, None),
            P("blk", None, None),
            P("blk", None),
            P("blk", None),
            P("blk", None),
        ),
        out_specs=P("blk", None, None),
        check_vma=False,
    )
```

```python
import functools

import jax
import jax.numpy as jnp
from jax import lax
from jax.experimental import pallas as pl
from jax.experimental.pallas import tpu as pltpu
from jax.sharding import PartitionSpec as P

BX = 256
LANES = 128
LEVELS = 32767.0
thresholds = (1.0, 0.8, 0.6, 0.5)
HALO = len(thresholds)
MESH = pl.DeviceIdType.MESH


def window(array, offset):
    shift = (LANES - offset) & (LANES - 1)
    parts = [
        pltpu.roll(array[:, LANES * j : LANES * (j + 1)], shift, 1)
        for j in range(BX // LANES + 1)
    ]
    lane = lax.broadcasted_iota(jnp.int32, parts[0].shape, 1)
    inside = lane < LANES - offset
    return jnp.concatenate(
        [jnp.where(inside, parts[j], parts[j + 1]) for j in range(BX // LANES)], axis=1
    )


def quotient(difference, square):
    bottom = square + difference * difference
    guess = pl.reciprocal(bottom, approx=True)
    return difference * (guess * (2.0 - bottom * guess))


def kernel(
    n, graw, gflat, gdark, gramp, gused, goff, out,
    raw, flat, dark, ramp, used, off,
    praw, pflat, pdark, pramp, fused, foff, nused, noff,
    corr, pcorr, qf, qn, rf, rn, sf, sn, rsf, rsn,
    qh, rh, sh, rsh, saved, u, local, send, recv,
):
    depth, rows = raw.shape[0], raw.shape[1]
    half = depth // 2
    me = lax.axis_index("blk")
    s = 2 * lax.rem(me, 2) - 1
    partner, near, far, far_from = me - s, me + s, me + 2 * s, me - 2 * s

    def inside(device):
        return jnp.logical_and(device >= 0, device < n)

    has_near, has_far, has_far_from = inside(near), inside(far), inside(far_from)
    has_below, has_above = me > 0, me < n - 1

    fetched = [
        pltpu.make_async_copy(source, target, local.at[number])
        for number, (source, target) in enumerate(
            ((gflat, flat), (gdark, dark), (graw, raw), (gramp, ramp), (gused, used), (goff, off))
        )
    ]
    for c in fetched:
        c.start()

    barrier = pltpu.get_barrier_semaphore()

    def greet(device):
        pl.semaphore_signal(barrier, inc=1, device_id=(device,), device_id_type=MESH)

    greet(partner)
    for device, there in ((near, has_near), (far, has_far), (far_from, has_far_from)):
        pl.when(there)(functools.partial(greet, device))
    pl.semaphore_wait(
        barrier,
        1
        + has_near.astype(jnp.int32)
        + has_far.astype(jnp.int32)
        + has_far_from.astype(jnp.int32),
    )

    def copy(number, source, target, device):
        return pltpu.make_async_remote_copy(
            src_ref=source,
            dst_ref=target,
            send_sem=send.at[number],
            recv_sem=recv.at[number],
            device_id=(device,),
            device_id_type=MESH,
        )

    meta_far = [copy(4, gused, fused, far_from), copy(5, goff, foff, far_from)]
    meta_near = [copy(6, gused, nused, near), copy(7, goff, noff, near)]
    tile = [
        copy(3, gramp, pramp, partner),
        copy(1, gflat, pflat, partner),
        copy(2, gdark, pdark, partner),
        copy(0, graw, praw, partner),
    ]

    def part(ref, chunk):
        return ref.at[pl.ds(chunk * half, half)]

    to_far = [copy(8 + c, part(qf, c), part(rf, c), far) for c in range(2)]
    to_far.append(copy(10, sf, rsf, far))
    to_near = [copy(11 + c, part(qn, c), part(rn, c), near) for c in range(2)]
    to_near.append(copy(13, sn, rsn, near))
    halos = [
        [copy(14, qh.at[0], rh.at[1], me - 1), copy(15, sh.at[0], rsh.at[1], me - 1)],
        [copy(16, qh.at[1], rh.at[0], me + 1), copy(17, sh.at[1], rsh.at[0], me + 1)],
    ]

    @pl.when(has_far_from)
    def _():
        for c in meta_far:
            c.start()

    @pl.when(has_near)
    def _():
        for c in meta_near:
            c.start()

    for c in tile:
        c.start()

    def corrected(raw_ref, flat_ref, dark_ref, target):
        inverse = 1.0 / flat_ref[0].astype(jnp.float32)
        level = dark_ref[0].astype(jnp.float32)

        def body(z, largest):
            value = (raw_ref[z].astype(jnp.float32) - level) * inverse
            target[z] = value
            return jnp.maximum(
                largest, jnp.max(jnp.abs(value).reshape(rows // 8, 8, -1), axis=0)
            )

        largest = lax.fori_loop(
            0, depth, body, jnp.zeros((8, raw_ref.shape[2]), jnp.float32)
        )
        return jnp.broadcast_to(
            jnp.max(largest, axis=0, keepdims=True), largest.shape
        )

    def weight(ramp_ref, taken, offset):
        row = jnp.broadcast_to(ramp_ref[...].astype(jnp.float32), (8, ramp_ref.shape[1]))
        return jnp.where(taken == 1, window(row, offset), 0.0)

    def levels(largest):
        return jnp.where(largest > 1e-30, LEVELS / jnp.maximum(largest, 1e-30), 0.0)

    def coded(value):
        return jnp.round(value).astype(jnp.int32).astype(jnp.int16)

    for c in fetched:
        c.wait()
    largest = corrected(raw, flat, dark, corr)

    def send_far(c):
        if c == 0:
            for received in meta_far:
                received.wait_recv()
        slot = 2 - 2 * s
        offset = foff[0, slot]
        scale = window(largest, offset)
        if c == 0:
            w = weight(ramp, fused[0, slot], offset)
            sf[0:8] = w * scale * (1.0 / LEVELS)
            sf[8:16] = w
            to_far[2].start()
        gain = levels(scale)[0:1]

        def body(z, _):
            qf[z] = coded(window(corr[z], offset) * gain)
            return 0

        lax.fori_loop(c * half, (c + 1) * half, body, 0)
        to_far[c].start()

    def send_near(c):
        if c == 0:
            for received in meta_near:
                received.wait_recv()
        own, other = 2 - s, 2 - 2 * s
        offset, poffset = noff[0, own], noff[0, other]
        w = weight(ramp, nused[0, own], offset)
        pw = weight(pramp, nused[0, other], poffset)
        total = w + pw
        scale = jnp.maximum(
            jnp.where(w > 0.0, window(largest, offset), 0.0),
            jnp.where(pw > 0.0, window(plargest, poffset), 0.0),
        )
        if c == 0:
            sn[0:8] = total * scale * (1.0 / LEVELS)
            sn[8:16] = total
            to_near[2].start()
        gain = levels(scale) / jnp.maximum(total, 1.0)
        a, b = (w * gain)[0:1], (pw * gain)[0:1]

        def body(z, _):
            qn[z] = coded(
                window(corr[z], offset) * a + window(pcorr[z], poffset) * b
            )
            return 0

        lax.fori_loop(c * half, (c + 1) * half, body, 0)
        to_near[c].start()

    pl.when(has_far)(functools.partial(send_far, 0))
    for c in tile:
        c.wait_recv()
    plargest = corrected(praw, pflat, pdark, pcorr)

    for c in range(2):
        pl.when(has_near)(functools.partial(send_near, c))
        if c == 0:
            pl.when(has_far)(functools.partial(send_far, 1))

    offset, poffset = off[0, 2], off[0, 2 - s]
    w = weight(ramp, used[0, 2], offset)
    pw = weight(pramp, used[0, 2 - s], poffset)
    a, b = w[0:1], pw[0:1]

    def base(z, _):
        u[HALO + z] = window(corr[z], offset) * a + window(pcorr[z], poffset) * b
        return 0

    lax.fori_loop(0, depth, base, 0)

    @pl.when(jnp.logical_not(has_far_from))
    def _():
        rsf[...] = jnp.zeros_like(rsf)

    @pl.when(jnp.logical_not(has_near))
    def _():
        rsn[...] = jnp.zeros_like(rsn)

    @pl.when(jnp.logical_not(has_below))
    def _():
        u[0:HALO] = jnp.zeros((HALO,) + u.shape[1:], jnp.float32)

    @pl.when(jnp.logical_not(has_above))
    def _():
        u[HALO + depth :] = jnp.zeros((HALO,) + u.shape[1:], jnp.float32)

    pl.when(has_far_from)(to_far[2].wait_recv)
    pl.when(has_near)(to_near[2].wait_recv)
    inverse = 1.0 / (w + pw + rsf[8:16] + rsn[8:16])
    scale_f = (rsf[0:8] * inverse)[0:1]
    scale_n = (rsn[0:8] * inverse)[0:1]
    inverse = inverse[0:1]
    for c in range(2):
        pl.when(has_far_from)(to_far[c].wait_recv)
        pl.when(has_near)(to_near[c].wait_recv)

        def join(z, largest):
            value = (
                u[HALO + z] * inverse
                + rf[z].astype(jnp.float32) * scale_f
                + rn[z].astype(jnp.float32) * scale_n
            )
            u[HALO + z] = value
            return jnp.maximum(
                largest, jnp.max(jnp.abs(value).reshape(rows // 8, 8, -1), axis=0)
            )

        largest = lax.fori_loop(
            c * half, (c + 1) * half, join, jnp.zeros((8, BX), jnp.float32)
        )

        @pl.when((has_below, has_above)[c])
        def _():
            scale = jnp.max(largest, axis=0, keepdims=True)
            sh[c] = jnp.broadcast_to(scale * (1.0 / LEVELS), (8, BX))
            gain = levels(scale)
            start = c * (depth - HALO)

            def code(z, _):
                qh[c, z] = coded(u[HALO + start + z] * gain)
                return 0

            lax.fori_loop(0, HALO, code, 0)
            for halo in halos[c]:
                halo.start()

    y = lax.broadcasted_iota(jnp.int32, u.shape[1:], 0)
    x = lax.broadcasted_iota(jnp.int32, u.shape[1:], 1)

    def stepped(here, before, after, square):
        step = pltpu.roll(here, rows - 1, 0) - here
        flow_y = quotient(jnp.where(y == rows - 1, 0.0, step), square)
        step = pltpu.roll(here, BX - 1, 1) - here
        flow_x = quotient(jnp.where(x == BX - 1, 0.0, step), square)
        flux = (
            (after - before)
            + (flow_y - pltpu.roll(flow_y, 1, 0))
            + (flow_x - pltpu.roll(flow_x, 1, 1))
        )
        return here + (0.12 * square) * flux

    planes = depth + 2 * HALO
    for number, kappa in enumerate(thresholds):
        square = kappa * kappa
        first, last = HALO + 1 + number, planes - HALO - 1 - number

        def body(z, before, square=square):
            here = u[z]
            after = quotient(u[z + 1] - here, square)
            u[z] = stepped(here, before, after, square)
            return after

        before = quotient(u[first] - u[first - 1], square)
        saved[0, number] = before
        saved[1, number] = -lax.fori_loop(
            first, last, body, before, unroll=True
        )

    lower_first = s > 0
    for turn in range(2):
        lower = lower_first if turn == 0 else jnp.logical_not(lower_first)
        side = jnp.where(lower, 0, 1)
        there = jnp.where(lower, has_below, has_above)
        origin = side * (planes - 1)
        sign = 1 - 2 * side

        @pl.when(jnp.logical_and(lower, has_below))
        def _():
            for halo in halos[1]:
                halo.wait_recv()

        @pl.when(jnp.logical_and(jnp.logical_not(lower), has_above))
        def _():
            for halo in halos[0]:
                halo.wait_recv()

        @pl.when(there)
        def _():
            scale = rsh[side, 0:1]

            def decode(z, _):
                u[side * (HALO + depth) + z] = rh[side, z].astype(jnp.float32) * scale
                return 0

            lax.fori_loop(0, HALO, decode, 0)

        open_face = jnp.where(there, 1.0, 0.0)
        for number, kappa in enumerate(thresholds):
            square = kappa * kappa
            final = number == HALO - 1

            def store(k, value, final=final):
                if final:
                    out[origin + sign * k - HALO] = value
                else:
                    u[origin + sign * k] = value

            def between(k, here, following, square=square):
                step = following - here
                return quotient(step * open_face if k == HALO - 1 else step, square)

            read = [u[origin + sign * (number + j)] for j in range(HALO + 1)]
            flows = [
                between(number + j, read[j], read[j + 1]) for j in range(HALO)
            ] + [saved[side, number]]
            values = [
                stepped(read[j], flows[j - 1], flows[j], square)
                for j in range(1, HALO + 1)
            ]
            for j, value in enumerate(values):
                store(number + 1 + j, value)

    @pl.when(has_below)
    def _():
        for halo in halos[0]:
            halo.wait_send()

    @pl.when(has_above)
    def _():
        for halo in halos[1]:
            halo.wait_send()

    for c in tile:
        c.wait_send()

    @pl.when(has_far_from)
    def _():
        for c in meta_far:
            c.wait_send()

    @pl.when(has_near)
    def _():
        for c in meta_near + to_near:
            c.wait_send()

    @pl.when(has_far)
    def _():
        for c in to_far:
            c.wait_send()


def shards(raw, flat, dark, ramp, used, off):
    n = lax.axis_size("blk")
    depth, rows, columns = raw.shape
    vmem = pl.BlockSpec(memory_space=pltpu.VMEM)
    coded = pltpu.VMEM((depth, rows, BX), jnp.int16)
    side = pltpu.VMEM((16, BX), jnp.float32)
    tile = pltpu.VMEM(raw.shape, jnp.float32)
    meta = pltpu.SMEM(used.shape, jnp.int32)
    held = [pltpu.VMEM(a.shape, a.dtype) for a in (raw, flat, dark, ramp)]
    return pl.pallas_call(
        functools.partial(kernel, n),
        out_shape=jax.ShapeDtypeStruct((depth, rows, BX), jnp.float32),
        in_specs=[pl.BlockSpec(memory_space=pl.ANY)] * 6,
        out_specs=vmem,
        scratch_shapes=[
            *held, meta, meta, *held, meta, meta, meta, meta,
            tile, tile, coded, coded, coded, coded, side, side, side, side,
            pltpu.VMEM((2, HALO, rows, BX), jnp.int16),
            pltpu.VMEM((2, HALO, rows, BX), jnp.int16),
            pltpu.VMEM((2, 8, BX), jnp.float32),
            pltpu.VMEM((2, 8, BX), jnp.float32),
            pltpu.VMEM((2, len(thresholds), rows, BX), jnp.float32),
            pltpu.VMEM((depth + 2 * HALO, rows, BX), jnp.float32),
            pltpu.SemaphoreType.DMA((6,)),
            pltpu.SemaphoreType.DMA((18,)),
            pltpu.SemaphoreType.DMA((18,)),
        ],
        compiler_params=pltpu.CompilerParams(
            collective_id=0, has_side_effects=True, vmem_limit_bytes=64 * 2**20 - 2**17
        ),
        cost_estimate=pl.CostEstimate(
            flops=30 * 6 * depth * rows * BX, bytes_accessed=10**6, transcendentals=0
        ),
    )(raw, flat, dark, ramp, used, off)


def solution(mesh):
    return jax.shard_map(
        shards,
        mesh=mesh,
        in_specs=(
            P("blk", None, None),
            P("blk", None, None),
            P("blk", None, None),
            P("blk", None),
            P("blk", None),
            P("blk", None),
        ),
        out_specs=P("blk", None, None),
        check_vma=False,
    )
```

```python
import functools

import jax
import jax.numpy as jnp
from jax import lax
from jax.experimental import pallas as pl
from jax.experimental.pallas import tpu as pltpu
from jax.sharding import PartitionSpec as P

BX = 256
LANES = 128
LEVELS = 32767.0
thresholds = (1.0, 0.8, 0.6, 0.5)
HALO = len(thresholds)
MESH = pl.DeviceIdType.MESH


def window(array, offset):
    shift = (LANES - offset) & (LANES - 1)
    parts = [
        pltpu.roll(array[:, LANES * j : LANES * (j + 1)], shift, 1)
        for j in range(BX // LANES + 1)
    ]
    lane = lax.broadcasted_iota(jnp.int32, parts[0].shape, 1)
    inside = lane < LANES - offset
    return jnp.concatenate(
        [jnp.where(inside, parts[j], parts[j + 1]) for j in range(BX // LANES)], axis=1
    )


def quotient(difference, square):
    bottom = square + difference * difference
    guess = pl.reciprocal(bottom, approx=True)
    return difference * (guess * (2.0 - bottom * guess))


def kernel(
    n, graw, gflat, gdark, gramp, gused, goff, out,
    raw, flat, dark, ramp, used, off,
    praw, pflat, pdark, pramp, fused, foff, nused, noff,
    corr, pcorr, qf, qn, rf, rn, sf, sn, rsf, rsn,
    qh, rh, sh, rsh, saved, u, local, send, recv,
):
    depth, rows = raw.shape[0], raw.shape[1]
    half = depth // 2
    me = lax.axis_index("blk")
    s = 2 * lax.rem(me, 2) - 1
    partner, near, far, far_from = me - s, me + s, me + 2 * s, me - 2 * s

    def inside(device):
        return jnp.logical_and(device >= 0, device < n)

    has_near, has_far, has_far_from = inside(near), inside(far), inside(far_from)
    has_below, has_above = me > 0, me < n - 1

    fetched = [
        pltpu.make_async_copy(source, target, local.at[number])
        for number, (source, target) in enumerate(
            ((gflat, flat), (gdark, dark), (graw, raw), (gramp, ramp), (gused, used), (goff, off))
        )
    ]
    for c in fetched:
        c.start()

    barrier = pltpu.get_barrier_semaphore()

    def greet(device):
        pl.semaphore_signal(barrier, inc=1, device_id=(device,), device_id_type=MESH)

    greet(partner)
    for device, there in ((near, has_near), (far, has_far), (far_from, has_far_from)):
        pl.when(there)(functools.partial(greet, device))
    pl.semaphore_wait(
        barrier,
        1
        + has_near.astype(jnp.int32)
        + has_far.astype(jnp.int32)
        + has_far_from.astype(jnp.int32),
    )

    def copy(number, source, target, device):
        return pltpu.make_async_remote_copy(
            src_ref=source,
            dst_ref=target,
            send_sem=send.at[number],
            recv_sem=recv.at[number],
            device_id=(device,),
            device_id_type=MESH,
        )

    meta_far = [copy(4, gused, fused, far_from), copy(5, goff, foff, far_from)]
    meta_near = [copy(6, gused, nused, near), copy(7, goff, noff, near)]
    tile = [
        copy(3, gramp, pramp, partner),
        copy(1, gflat, pflat, partner),
        copy(2, gdark, pdark, partner),
        copy(0, graw, praw, partner),
    ]

    def part(ref, chunk):
        return ref.at[pl.ds(chunk * half, half)]

    to_far = [copy(8 + c, part(qf, c), part(rf, c), far) for c in range(2)]
    to_far.append(copy(10, sf, rsf, far))
    to_near = [copy(11 + c, part(qn, c), part(rn, c), near) for c in range(2)]
    to_near.append(copy(13, sn, rsn, near))
    halos = [
        [copy(14, qh.at[0], rh.at[1], me - 1), copy(15, sh.at[0], rsh.at[1], me - 1)],
        [copy(16, qh.at[1], rh.at[0], me + 1), copy(17, sh.at[1], rsh.at[0], me + 1)],
    ]

    @pl.when(has_far_from)
    def _():
        for c in meta_far:
            c.start()

    @pl.when(has_near)
    def _():
        for c in meta_near:
            c.start()

    for c in tile:
        c.start()

    def corrected(raw_ref, flat_ref, dark_ref, target):
        inverse = 1.0 / flat_ref[0].astype(jnp.float32)
        level = dark_ref[0].astype(jnp.float32)

        def body(z, largest):
            value = (raw_ref[z].astype(jnp.float32) - level) * inverse
            target[z] = value
            return jnp.maximum(
                largest, jnp.max(jnp.abs(value).reshape(rows // 8, 8, -1), axis=0)
            )

        largest = lax.fori_loop(
            0, depth, body, jnp.zeros((8, raw_ref.shape[2]), jnp.float32)
        )
        return jnp.broadcast_to(
            jnp.max(largest, axis=0, keepdims=True), largest.shape
        )

    def weight(ramp_ref, taken, offset):
        row = jnp.broadcast_to(ramp_ref[...].astype(jnp.float32), (8, ramp_ref.shape[1]))
        return jnp.where(taken == 1, window(row, offset), 0.0)

    def levels(largest):
        return jnp.where(largest > 1e-30, LEVELS / jnp.maximum(largest, 1e-30), 0.0)

    def coded(value):
        return jnp.round(value).astype(jnp.int32).astype(jnp.int16)

    for c in fetched:
        c.wait()
    largest = corrected(raw, flat, dark, corr)

    def send_far(c):
        if c == 0:
            for received in meta_far:
                received.wait_recv()
        slot = 2 - 2 * s
        offset = foff[0, slot]
        scale = window(largest, offset)
        if c == 0:
            w = weight(ramp, fused[0, slot], offset)
            sf[0:8] = w * scale * (1.0 / LEVELS)
            sf[8:16] = w
            to_far[2].start()
        gain = levels(scale)[0:1]

        def body(z, _):
            qf[z] = coded(window(corr[z], offset) * gain)
            return 0

        lax.fori_loop(c * half, (c + 1) * half, body, 0, unroll=2)
        to_far[c].start()

    def send_near(c):
        if c == 0:
            for received in meta_near:
                received.wait_recv()
        own, other = 2 - s, 2 - 2 * s
        offset, poffset = noff[0, own], noff[0, other]
        w = weight(ramp, nused[0, own], offset)
        pw = weight(pramp, nused[0, other], poffset)
        total = w + pw
        scale = jnp.maximum(
            jnp.where(w > 0.0, window(largest, offset), 0.0),
            jnp.where(pw > 0.0, window(plargest, poffset), 0.0),
        )
        if c == 0:
            sn[0:8] = total * scale * (1.0 / LEVELS)
            sn[8:16] = total
            to_near[2].start()
        gain = levels(scale) / jnp.maximum(total, 1.0)
        a, b = (w * gain)[0:1], (pw * gain)[0:1]

        def body(z, _):
            qn[z] = coded(
                window(corr[z], offset) * a + window(pcorr[z], poffset) * b
            )
            return 0

        lax.fori_loop(c * half, (c + 1) * half, body, 0, unroll=2)
        to_near[c].start()

    pl.when(has_far)(functools.partial(send_far, 0))
    for c in tile:
        c.wait_recv()
    plargest = corrected(praw, pflat, pdark, pcorr)

    for c in range(2):
        pl.when(has_near)(functools.partial(send_near, c))
        if c == 0:
            pl.when(has_far)(functools.partial(send_far, 1))

    offset, poffset = off[0, 2], off[0, 2 - s]
    w = weight(ramp, used[0, 2], offset)
    pw = weight(pramp, used[0, 2 - s], poffset)
    a, b = w[0:1], pw[0:1]

    def base(z, _):
        u[HALO + z] = window(corr[z], offset) * a + window(pcorr[z], poffset) * b
        return 0

    lax.fori_loop(0, depth, base, 0, unroll=2)

    @pl.when(jnp.logical_not(has_far_from))
    def _():
        rsf[...] = jnp.zeros_like(rsf)

    @pl.when(jnp.logical_not(has_near))
    def _():
        rsn[...] = jnp.zeros_like(rsn)

    @pl.when(jnp.logical_not(has_below))
    def _():
        u[0:HALO] = jnp.zeros((HALO,) + u.shape[1:], jnp.float32)

    @pl.when(jnp.logical_not(has_above))
    def _():
        u[HALO + depth :] = jnp.zeros((HALO,) + u.shape[1:], jnp.float32)

    pl.when(has_far_from)(to_far[2].wait_recv)
    pl.when(has_near)(to_near[2].wait_recv)
    inverse = 1.0 / (w + pw + rsf[8:16] + rsn[8:16])
    scale_f = (rsf[0:8] * inverse)[0:1]
    scale_n = (rsn[0:8] * inverse)[0:1]
    inverse = inverse[0:1]
    for c in range(2):
        pl.when(has_far_from)(to_far[c].wait_recv)
        pl.when(has_near)(to_near[c].wait_recv)

        def join(z, largest):
            value = (
                u[HALO + z] * inverse
                + rf[z].astype(jnp.float32) * scale_f
                + rn[z].astype(jnp.float32) * scale_n
            )
            u[HALO + z] = value
            return jnp.maximum(
                largest, jnp.max(jnp.abs(value).reshape(rows // 8, 8, -1), axis=0)
            )

        largest = lax.fori_loop(
            c * half, (c + 1) * half, join, jnp.zeros((8, BX), jnp.float32)
        )

        @pl.when((has_below, has_above)[c])
        def _():
            scale = jnp.max(largest, axis=0, keepdims=True)
            sh[c] = jnp.broadcast_to(scale * (1.0 / LEVELS), (8, BX))
            gain = levels(scale)
            start = c * (depth - HALO)

            def code(z, _):
                qh[c, z] = coded(u[HALO + start + z] * gain)
                return 0

            lax.fori_loop(0, HALO, code, 0)
            for halo in halos[c]:
                halo.start()

    y = lax.broadcasted_iota(jnp.int32, u.shape[1:], 0)
    x = lax.broadcasted_iota(jnp.int32, u.shape[1:], 1)

    def stepped(here, before, after, square):
        step = pltpu.roll(here, rows - 1, 0) - here
        flow_y = quotient(jnp.where(y == rows - 1, 0.0, step), square)
        step = pltpu.roll(here, BX - 1, 1) - here
        flow_x = quotient(jnp.where(x == BX - 1, 0.0, step), square)
        flux = (
            (after - before)
            + (flow_y - pltpu.roll(flow_y, 1, 0))
            + (flow_x - pltpu.roll(flow_x, 1, 1))
        )
        return here + (0.12 * square) * flux

    planes = depth + 2 * HALO
    for number, kappa in enumerate(thresholds):
        square = kappa * kappa
        first, last = HALO + 1 + number, planes - HALO - 1 - number

        def body(z, before, square=square):
            here = u[z]
            after = quotient(u[z + 1] - here, square)
            u[z] = stepped(here, before, after, square)
            return after

        before = quotient(u[first] - u[first - 1], square)
        saved[0, number] = before
        saved[1, number] = -lax.fori_loop(
            first, last, body, before, unroll=True
        )

    lower_first = s > 0
    for turn in range(2):
        lower = lower_first if turn == 0 else jnp.logical_not(lower_first)
        side = jnp.where(lower, 0, 1)
        there = jnp.where(lower, has_below, has_above)
        origin = side * (planes - 1)
        sign = 1 - 2 * side

        @pl.when(jnp.logical_and(lower, has_below))
        def _():
            for halo in halos[1]:
                halo.wait_recv()

        @pl.when(jnp.logical_and(jnp.logical_not(lower), has_above))
        def _():
            for halo in halos[0]:
                halo.wait_recv()

        @pl.when(there)
        def _():
            scale = rsh[side, 0:1]

            def decode(z, _):
                u[side * (HALO + depth) + z] = rh[side, z].astype(jnp.float32) * scale
                return 0

            lax.fori_loop(0, HALO, decode, 0)

        open_face = jnp.where(there, 1.0, 0.0)
        for number, kappa in enumerate(thresholds):
            square = kappa * kappa
            final = number == HALO - 1

            def store(k, value, final=final):
                if final:
                    out[origin + sign * k - HALO] = value
                else:
                    u[origin + sign * k] = value

            def between(k, here, following, square=square):
                step = following - here
                return quotient(step * open_face if k == HALO - 1 else step, square)

            read = [u[origin + sign * (number + j)] for j in range(HALO + 1)]
            flows = [
                between(number + j, read[j], read[j + 1]) for j in range(HALO)
            ] + [saved[side, number]]
            values = [
                stepped(read[j], flows[j - 1], flows[j], square)
                for j in range(1, HALO + 1)
            ]
            for j, value in enumerate(values):
                store(number + 1 + j, value)

    @pl.when(has_below)
    def _():
        for halo in halos[0]:
            halo.wait_send()

    @pl.when(has_above)
    def _():
        for halo in halos[1]:
            halo.wait_send()

    for c in tile:
        c.wait_send()

    @pl.when(has_far_from)
    def _():
        for c in meta_far:
            c.wait_send()

    @pl.when(has_near)
    def _():
        for c in meta_near + to_near:
            c.wait_send()

    @pl.when(has_far)
    def _():
        for c in to_far:
            c.wait_send()


def shards(raw, flat, dark, ramp, used, off):
    n = lax.axis_size("blk")
    depth, rows, columns = raw.shape
    vmem = pl.BlockSpec(memory_space=pltpu.VMEM)
    coded = pltpu.VMEM((depth, rows, BX), jnp.int16)
    side = pltpu.VMEM((16, BX), jnp.float32)
    tile = pltpu.VMEM(raw.shape, jnp.float32)
    meta = pltpu.SMEM(used.shape, jnp.int32)
    held = [pltpu.VMEM(a.shape, a.dtype) for a in (raw, flat, dark, ramp)]
    return pl.pallas_call(
        functools.partial(kernel, n),
        out_shape=jax.ShapeDtypeStruct((depth, rows, BX), jnp.float32),
        in_specs=[pl.BlockSpec(memory_space=pl.ANY)] * 6,
        out_specs=vmem,
        scratch_shapes=[
            *held, meta, meta, *held, meta, meta, meta, meta,
            tile, tile, coded, coded, coded, coded, side, side, side, side,
            pltpu.VMEM((2, HALO, rows, BX), jnp.int16),
            pltpu.VMEM((2, HALO, rows, BX), jnp.int16),
            pltpu.VMEM((2, 8, BX), jnp.float32),
            pltpu.VMEM((2, 8, BX), jnp.float32),
            pltpu.VMEM((2, len(thresholds), rows, BX), jnp.float32),
            pltpu.VMEM((depth + 2 * HALO, rows, BX), jnp.float32),
            pltpu.SemaphoreType.DMA((6,)),
            pltpu.SemaphoreType.DMA((18,)),
            pltpu.SemaphoreType.DMA((18,)),
        ],
        compiler_params=pltpu.CompilerParams(
            collective_id=0, has_side_effects=True, vmem_limit_bytes=64 * 2**20 - 2**17
        ),
        cost_estimate=pl.CostEstimate(
            flops=30 * 6 * depth * rows * BX, bytes_accessed=10**6, transcendentals=0
        ),
    )(raw, flat, dark, ramp, used, off)


def solution(mesh):
    return jax.shard_map(
        shards,
        mesh=mesh,
        in_specs=(
            P("blk", None, None),
            P("blk", None, None),
            P("blk", None, None),
            P("blk", None),
            P("blk", None),
            P("blk", None),
        ),
        out_specs=P("blk", None, None),
        check_vma=False,
    )
```
